32 devices in a mesh: gx: 2 (over x), gy: 4 (over z), gz: 4 (over y, core).
Axes of the slice: x: 2, y: 2, z: 4, core: 2. Of those that a mesh axis runs over, the one named last changes fastest.
Arguments:
- coeffs: float32 [32, 512, 512], P(('gx', 'gy', 'gz')), may hold values from -6 to 6
- transfer: float32 [4, 32, 512, 1024], P(None, ('gx', 'gy', 'gz')), may hold values from -0.1875 to 0.1875
Outputs:
- result: float32 [32, 512, 512], P(('gx', 'gy', 'gz'))
The draws below stay inside these ranges and needn't reach their ends.
All inputs are finite; a program needn't handle non-finite values.
Results may differ from the reference program's by a relative error of at most 0.0001.
Values sent between devices are 32-bit elements; how exact they have to be, the bound alone decides.
No kernel may reach another device: no remote copies, remote signals or barrier semaphores. Data moves between devices by JAX's collectives and lax.ppermute only.
A program may use at most 64 MiB of HBM per device.

```python
import jax
import jax.numpy as jnp
from jax import lax

RANK = 512
RHS = 512
LEVELS = 4
BOXES = 32


def block_levels(own_key, dims, cuts, smallest, largest):
    loudness = 1.0
    for axis_at, blocks in cuts:
        steps = jax.random.uniform(jax.random.fold_in(jax.random.fold_in(own_key, 6), axis_at), (blocks,), jnp.float32, smallest / len(cuts), largest / len(cuts))
        loudness = loudness * jnp.repeat(jnp.exp(steps), dims[axis_at] // blocks).reshape((-1,) + (1,) * (len(dims) - 1 - axis_at))
    return loudness


def centred(key, extent, spread, most, cuts=(), dtype=jnp.bfloat16):
    factor_of = block_levels(key, extent, cuts, -0.22, 0.18) if cuts else 1.0
    array = jax.random.normal(key, extent, jnp.float32) * spread * factor_of
    return jnp.minimum(jnp.maximum(array, -most), most).astype(dtype)


def setup_inputs(seed: int = 0) -> dict:
    arg_keys = jax.random.split(jax.random.key(seed), 3)
    return {
        "coeffs": centred(arg_keys[0], (BOXES, RANK, RHS), 1.0, 6.0, ((0, 32),), jnp.float32),
        "transfer": centred(arg_keys[1], (LEVELS, BOXES, RANK, 2 * RANK), (2 * RANK) ** -0.5, 0.1875, ((1, 32),), jnp.float32),
    }


def reference(coeffs, transfer):
    count = coeffs.shape[0]
    nbits = count.bit_length() - 1
    current = coeffs
    for level in range(LEVELS):
        span = 2 ** (nbits - 1 - level)
        grouped = current.reshape(count // (2 * span), 2, span, RANK, RHS)
        paired = jnp.concatenate([grouped[:, 0], grouped[:, 1]], axis=2)
        paired = jnp.stack([paired, paired], axis=1).reshape(count, 2 * RANK, RHS)
        current = jnp.einsum("prs,psk->prk", transfer[level], paired, precision=lax.Precision.HIGHEST)
    return current
```

```python
import jax
import jax.numpy as jnp
from jax import lax
from jax.experimental import pallas as pl
from jax.experimental.pallas import tpu as pltpu
from jax.sharding import PartitionSpec as P

AXES = ("gx", "gy", "gz")
F32, BF16 = jnp.float32, jnp.bfloat16
VMEM = pl.BlockSpec(memory_space=pltpu.VMEM)
HBM = pl.BlockSpec(memory_space=pltpu.HBM)
ANY = pl.BlockSpec(memory_space=pl.ANY)
CHUNKS = (2, 3, 3, 4, 4)
X_GROUPS = ((0,), (1,), (2,), (3,), (4,))
Z_GROUPS = ((0,), (1,), (2,), (3,), (4,))
Y_GROUPS = ((0,), (1,), (2,), (3,), (4,))
DIRECT = (0,)
RESULT_BLOCKS = ((0, 3), (3, 4))
COST = 4000000000
ORDER = (
    "in0 x0 in1 x1",
    "x2 m0 a0 m2",
    "x3 x4 m1 a1",
    "a2 b0 p1 a3",
    "p2 a4 q1 p3",
    "p4 m3 q2 q3",
    "c0 b1 q4 b2",
    "c1 b3 c2 b4",
    "c3 c4 d0 d1",
)


def bit_of(bit):
    index = lax.axis_index(AXES[0])
    for axis in AXES[1:]:
        index = index * lax.axis_size(axis) + lax.axis_index(axis)
    return index >> bit & 1


def send(block, partner):
    count = lax.axis_size(AXES)
    return lax.ppermute(block, AXES, [(i, partner(i)) for i in range(count)])


def split(x):
    high = x.astype(BF16)
    return high, (x - high.astype(F32)).astype(BF16)


def dot_t(a, b):
    return lax.dot_general(a, b, (((1,), (1,)), ((), ())), preferred_element_type=F32)


def product(x, mh, ml):
    rows = x.shape[0]
    xh, xl = split(x)
    both = dot_t(jnp.concatenate([xh, xl], axis=0), mh)
    return both[:rows] + (both[rows:] + dot_t(xh, ml))


def product_t(x, mh, ml):
    rows = x.shape[0]
    xh, xl = split(x)
    both = dot_t(mh, jnp.concatenate([xh, xl], axis=0))
    return both[:, :rows] + (both[:, rows:] + dot_t(ml, xh))


def stacked(own, other, upper):
    return jnp.concatenate(
        [jnp.where(upper == 1, other, own), jnp.where(upper == 1, own, other)], axis=1
    )


def joined(blocks):
    return blocks[0] if len(blocks) == 1 else jnp.concatenate(blocks, axis=0)


class Chain:
    def __init__(self):
        self.last = None

    def __call__(self, name, body, args, outs, scratch=(), in_place=None, in_hbm=(), out_hbm=False):
        args, n = list(args), len(args)
        specs = [VMEM] * n
        for i in in_hbm:
            args[i] = pltpu.with_memory_space_constraint(args[i], pltpu.HBM)
            specs[i] = HBM
        if in_place is not None:
            specs[in_place] = HBM if out_hbm else ANY
        if self.last is not None and not any(a is self.last for a in args):
            args.append(self.last)
            specs.append(ANY)

        def kernel(*refs):
            body(*refs[:n], *refs[len(args) :])

        results = pl.pallas_call(
            kernel,
            out_shape=outs,
            in_specs=specs,
            out_specs=[HBM, VMEM] if out_hbm else [VMEM if in_place is None else ANY] * len(outs),
            scratch_shapes=scratch,
            input_output_aliases={} if in_place is None else {in_place: 0},
            compiler_params=pltpu.CompilerParams(vmem_limit_bytes=8 * 2**20),
            cost_estimate=pl.CostEstimate(
                flops=COST, bytes_accessed=1000, transcendentals=0
            ),
            name=name,
        )(*args)
        self.last = results[-1]
        return list(results)


def per_device(coeffs, transfer):
    nbits = lax.axis_size(AXES).bit_length() - 1
    bits = [nbits - 1 - level for level in range(transfer.shape[0])]
    rank, rhs = coeffs.shape[1:]
    sizes = [c * rhs // 16 for c in CHUNKS]
    n = len(sizes)
    ends = [sum(sizes[: s + 1]) for s in range(n)]
    unit = rhs // 4
    chain = Chain()

    def rows(chunks):
        return jax.ShapeDtypeStruct((sum(sizes[k] for k in chunks), rank), F32)

    def across(level):
        return lambda i: i ^ 1 << bits[level]

    def middle(i):
        both = 1 << bits[1] | 1 << bits[2]
        return i ^ both if (i >> bits[1] ^ i >> bits[2]) & 1 else i ^ 1

    def is_middle():
        return bit_of(bits[1]) != bit_of(bits[2])

    def pieces(store, chunks):
        found = []
        for group, array in store.items():
            at = 0
            for k in group:
                if k in chunks:
                    if found and found[-1][0] is array:
                        found[-1][1][1] = at + sizes[k]
                    else:
                        found.append((array, [at, at + sizes[k]]))
                at += sizes[k]
        return found

    def step_in(part):
        mine = [g for i, g in enumerate(X_GROUPS) if (i == 0) == (part == 0)]
        start = ends[mine[0][0]] - sizes[mine[0][0]]
        width = sum(sizes[k] for g in mine for k in g)
        low = start // 128 * 128
        high = -(-(start + width) // 128) * 128

        def fetched(c_ref, *refs):
            outs, (held, sem) = refs[:-2], refs[-2:]
            copy = pltpu.make_async_copy(c_ref.at[0, :, low:high], held, sem)
            copy.start()
            copy.wait()
            lay(held[...], start - low, outs)

        def whole(c_ref, *outs):
            lay(c_ref[0], start, outs)

        def lay(block, at, outs):
            for o_ref in outs:
                o_ref[...] = block[:, at : at + o_ref.shape[0]].T
                at += o_ref.shape[0]

        scratch = [pltpu.VMEM((rank, high - low), F32), pltpu.SemaphoreType.DMA]
        out = chain(
            "columns",
            whole if part else fetched,
            [coeffs],
            [rows(g) for g in mine],
            scratch=[] if part else scratch,
            in_hbm=[] if part else [0],
        )
        c0.update(zip(mine, out))

    def step_m(level):
        def body(t_ref, h_ref, l_ref):
            h_ref[...], l_ref[...] = split(t_ref[level, 0])

        matrix[level] = chain(
            "matrix",
            body,
            [transfer],
            [jax.ShapeDtypeStruct((rank, 2 * rank), BF16)] * 2,
        )

    def step_x(i):
        group = X_GROUPS[i]
        c0[group] = chain("order", lambda *_: None, [c0[group]], [rows(group)], in_place=0)[0]
        x[group] = send(c0[group], across(0))

    def level(name, number, mine, other, outs):
        args = [p[0] for p in mine] + [a for p in other for a in p[:-1]]

        def body(*refs):
            out_refs = refs[len(args) + 2 :]
            h, l = refs[len(args) : len(args) + 2]
            own = joined([r[slice(*p[-1])] for r, p in zip(refs, mine)])
            at, blocks = len(mine), []
            for p in other:
                block = refs[at][slice(*p[-1])]
                if len(p) == 3:
                    block = jnp.where(is_middle(), block, refs[at + 1][slice(*p[-1])])
                at += len(p) - 1
                blocks.append(block)
            y = product(stacked(own, joined(blocks), bit_of(bits[number])), h[...], l[...])
            at = 0
            for o in out_refs:
                o[...] = y[at : at + o.shape[0]]
                at += o.shape[0]

        return chain(name, body, args + matrix[number], outs)

    def step_a(i):
        group = X_GROUPS[i]
        out = level(
            "level0",
            0,
            pieces(c0, group),
            pieces(x, group),
            [rows([k]) for k in group],
        )
        for k, c in zip(group, out):
            c1[(k,)] = c
            if k in DIRECT:
                got[k] = (send(c, across(1)),)
            else:
                got[k] = send(c, middle)

    def step_p(k):
        def body(own, other, o_ref):
            o_ref[...] = jnp.where(is_middle(), other[...], own[...])

        passed = chain("pass", body, [c1[(k,)], got[k]], [rows([k])])[0]
        got[k] = send(passed, across(2))

    def step_q(k):
        kept = chain("order", lambda *_: None, [got[k]], [rows([k])], in_place=0)[0]
        got[k] = (send(kept, middle), kept)

    def step_b(i):
        group = Z_GROUPS[i]
        other = [(*got[k], [0, sizes[k]]) for k in group]
        c2[group] = level("level1", 1, pieces(c1, group), other, [rows(group)])[0]
        z[group] = send(c2[group], across(2))

    def step_c(i):
        group = Y_GROUPS[i]
        c3[group] = level("level2", 2, pieces(c2, group), pieces(z, group), [rows(group)])[0]
        y[group] = send(c3[group], across(3))

    def step_d(j):
        first, stop = (b * unit for b in RESULT_BLOCKS[j])
        args, cuts = [], []
        for store in (c3, y):
            for group in Y_GROUPS:
                begin = ends[group[0]] - sizes[group[0]]
                cut = slice(max(first - begin, 0), min(stop, ends[group[-1]]) - begin)
                if cut.start < cut.stop:
                    args.append(store[group])
                    cuts.append(cut)
        p = len(args) // 2

        def body(*refs):
            held, sem = refs[-2:]
            h, l, o_ref, mark = refs[2 * p], refs[2 * p + 1], refs[-4], refs[-3]
            mark[...] = jnp.zeros_like(mark)
            own = joined([r[cut] for r, cut in zip(refs[:p], cuts)])
            other = joined([r[cut] for r, cut in zip(refs[p:], cuts[p:])])
            both = stacked(own, other, bit_of(bits[3]))
            copies = []
            for half in range(2):
                part = slice(half * rank // 2, (half + 1) * rank // 2)
                held[part] = product_t(both, h[part], l[part])
                copies.append(
                    pltpu.make_async_copy(
                        held.at[part], o_ref.at[0, part, first:stop], sem.at[half]
                    )
                )
                copies[-1].start()
            for copy in copies:
                copy.wait()

        args += matrix[3]
        in_place = None
        if result:
            in_place = len(args)
            args.append(result[-1])
        result.append(
            chain(
                "level3",
                body,
                args,
                [pltpu.HBM(coeffs.shape, F32), jax.ShapeDtypeStruct((8, 128), F32)],
                scratch=[
                    pltpu.VMEM((rank, stop - first), F32),
                    pltpu.SemaphoreType.DMA((2,)),
                ],
                in_place=in_place,
                out_hbm=True,
            )[0]
        )

    c0, x, c1, got, c2, z, c3, y, matrix, result = ({} for _ in range(10))
    result = []
    steps = {"in": step_in, "m": step_m, "x": step_x, "a": step_a, "p": step_p}
    steps |= {"q": step_q, "b": step_b, "c": step_c, "d": step_d}
    for words in ORDER:
        for word in words.split():
            steps[word[:-1]](int(word[-1]))
    return result[-1]


def solution(mesh):
    placed = (P(AXES, None, None), P(None, AXES, None, None))
    return jax.shard_map(
        per_device,
        mesh=mesh,
        in_specs=placed,
        out_specs=P(AXES, None, None),
        check_vma=False,
    )
```

```python
import jax
import jax.numpy as jnp
from jax import lax
from jax.experimental import pallas as pl
from jax.experimental.pallas import tpu as pltpu
from jax.sharding import PartitionSpec as P

AXES = ("gx", "gy", "gz")
F32, BF16 = jnp.float32, jnp.bfloat16
VMEM = pl.BlockSpec(memory_space=pltpu.VMEM)
HBM = pl.BlockSpec(memory_space=pltpu.HBM)
ANY = pl.BlockSpec(memory_space=pl.ANY)
CHUNKS = (4, 6, 6, 8, 8)
X_GROUPS = ((0,), (1,), (2,), (3,), (4,))
S_GROUPS = ((0,), (1,), (2,), (3,), (4,))
B_GROUPS = ((0,), (1,), (2,), (3,), (4,))
Z_GROUPS = ((0,), (1,), (2,), (3,), (4,))
Y_GROUPS = ((0,), (1,), (2,), (3,), (4,))
DIRECT = (0,)
RESULT_BLOCKS = ((0, 3), (3, 4))
COST = 4000000000
COSTS = {}
ORDER = (
    "in0 x0 in1 x1",
    "x2 m0 a0 x3",
    "m1 x4 m2 a1",
    "a2 b0 p1 a3",
    "p2 a4 p3 q1",
    "p4 m3 q2 q3",
    "c0 b1 q4 b2",
    "c1 b3 c2 b4",
    "cc4 c3 c4 d0",
    "dd1 d1",
)


def bit_of(bit):
    index = lax.axis_index(AXES[0])
    for axis in AXES[1:]:
        index = index * lax.axis_size(axis) + lax.axis_index(axis)
    return index >> bit & 1


def send(block, partner):
    count = lax.axis_size(AXES)
    return lax.ppermute(block, AXES, [(i, partner(i)) for i in range(count)])


def split(x):
    high = x.astype(BF16)
    return high, (x - high.astype(F32)).astype(BF16)


def dot_t(a, b):
    return lax.dot_general(a, b, (((1,), (1,)), ((), ())), preferred_element_type=F32)


def product(x, mh, ml):
    rows = x.shape[0]
    xh, xl = split(x)
    both = dot_t(jnp.concatenate([xh, xl], axis=0), mh)
    return both[:rows] + (both[rows:] + dot_t(xh, ml))


def product_t(x, mh, ml):
    rows = x.shape[0]
    xh, xl = split(x)
    both = dot_t(mh, jnp.concatenate([xh, xl], axis=0))
    return both[:, :rows] + (both[:, rows:] + dot_t(ml, xh))


def stacked(own, other, upper):
    return jnp.concatenate(
        [jnp.where(upper == 1, other, own), jnp.where(upper == 1, own, other)], axis=1
    )


def joined(blocks):
    return blocks[0] if len(blocks) == 1 else jnp.concatenate(blocks, axis=0)


class Chain:
    def __init__(self):
        self.last = None

    def __call__(self, name, body, args, outs, scratch=(), in_place=None, in_hbm=(), out_hbm=False):
        args, n = list(args), len(args)
        specs = [VMEM] * n
        for i in in_hbm:
            args[i] = pltpu.with_memory_space_constraint(args[i], pltpu.HBM)
            specs[i] = HBM
        if in_place is not None:
            specs[in_place] = HBM if out_hbm else ANY
        if self.last is not None and not any(a is self.last for a in args):
            args.append(self.last)
            specs.append(ANY)

        def kernel(*refs):
            body(*refs[:n], *refs[len(args) :])

        results = pl.pallas_call(
            kernel,
            out_shape=outs,
            in_specs=specs,
            out_specs=[HBM, VMEM] if out_hbm else [VMEM if in_place is None else ANY] * len(outs),
            scratch_shapes=scratch,
            input_output_aliases={} if in_place is None else {in_place: 0},
            compiler_params=pltpu.CompilerParams(vmem_limit_bytes=8 * 2**20),
            cost_estimate=pl.CostEstimate(
                flops=COSTS.get(name, COST), bytes_accessed=1000, transcendentals=0
            ),
            name=name,
        )(*args)
        self.last = results[-1]
        return list(results)


def per_device(coeffs, transfer):
    nbits = lax.axis_size(AXES).bit_length() - 1
    bits = [nbits - 1 - level for level in range(transfer.shape[0])]
    rank, rhs = coeffs.shape[1:]
    sizes = [c * rhs // 32 for c in CHUNKS]
    n = len(sizes)
    ends = [sum(sizes[: s + 1]) for s in range(n)]
    unit = rhs // 4
    chain = Chain()

    def rows(chunks):
        return jax.ShapeDtypeStruct((sum(sizes[k] for k in chunks), rank), F32)

    def across(level):
        return lambda i: i ^ 1 << bits[level]

    def middle(i):
        both = 1 << bits[1] | 1 << bits[2]
        return i ^ both if (i >> bits[1] ^ i >> bits[2]) & 1 else i ^ 1

    def is_middle():
        return bit_of(bits[1]) != bit_of(bits[2])

    def pieces(store, chunks):
        found = []
        for group in sorted(store):
            arrays = store[group]
            arrays = arrays if isinstance(arrays, tuple) else (arrays,)
            at = 0
            for k in group:
                if k in chunks:
                    if found and found[-1][0] is arrays[0]:
                        found[-1][-1][1] = at + sizes[k]
                    else:
                        found.append((*arrays, [at, at + sizes[k]]))
                at += sizes[k]
        return found

    def step_in(part):
        mine = [g for i, g in enumerate(X_GROUPS) if (i == 0) == (part == 0)]
        start = ends[mine[0][0]] - sizes[mine[0][0]]
        width = sum(sizes[k] for g in mine for k in g)
        low = start // 128 * 128
        high = -(-(start + width) // 128) * 128

        def fetched(c_ref, *refs):
            outs, (held, sem) = refs[:-2], refs[-2:]
            copy = pltpu.make_async_copy(c_ref.at[0, :, low:high], held, sem)
            copy.start()
            copy.wait()
            lay(held[...], start - low, outs)

        def whole(c_ref, *outs):
            lay(c_ref[0], start, outs)

        def lay(block, at, outs):
            for o_ref in outs:
                o_ref[...] = block[:, at : at + o_ref.shape[0]].T
                at += o_ref.shape[0]

        scratch = [pltpu.VMEM((rank, high - low), F32), pltpu.SemaphoreType.DMA]
        out = chain(
            "columns",
            whole if part else fetched,
            [coeffs],
            [rows(g) for g in mine],
            scratch=[] if part else scratch,
            in_hbm=[] if part else [0],
        )
        c0.update(zip(mine, out))

    def step_m(level):
        def body(t_ref, h_ref, l_ref):
            h_ref[...], l_ref[...] = split(t_ref[level, 0])

        matrix[level] = chain(
            "matrix",
            body,
            [transfer],
            [jax.ShapeDtypeStruct((rank, 2 * rank), BF16)] * 2,
        )

    def step_x(i):
        group = X_GROUPS[i]
        c0[group] = chain("order", lambda *_: None, [c0[group]], [rows(group)], in_place=0)[0]
        x[group] = send(c0[group], across(0))

    def own_half(ref, number):
        upper = bit_of(bits[number])
        own = ref[:, pl.ds(pl.multiple_of(upper * rank, rank), rank)]
        return own, ref[:, pl.ds(pl.multiple_of((1 - upper) * rank, rank), rank)]

    def ahead(key, number, mine, turned=False):
        args = [p[0] for p in mine]
        size = sum(p[-1][1] - p[-1][0] for p in mine)

        def body(*refs):
            h, l, o = refs[len(args) :]
            own = joined([r[slice(*p[-1])] for r, p in zip(refs, mine)])
            times = product_t if turned else product
            o[...] = times(own, own_half(h, number)[0], own_half(l, number)[0])

        shape = (rank, size) if turned else (size, rank)
        outs = [jax.ShapeDtypeStruct(shape, F32)]
        done[key] = chain("ahead", body, args + matrix[number], outs)[0]

    def level(name, number, mine, other, outs, key=None):
        if key in done:
            mine = [(done[key], [0, sum(p[-1][1] - p[-1][0] for p in mine)])]
        args = [p[0] for p in mine] + [a for p in other for a in p[:-1]]

        def body(*refs):
            out_refs = refs[len(args) + 2 :]
            h, l = refs[len(args) : len(args) + 2]
            own = joined([r[slice(*p[-1])] for r, p in zip(refs, mine)])
            at, blocks = len(mine), []
            for p in other:
                block = refs[at][slice(*p[-1])]
                if len(p) == 3:
                    block = jnp.where(is_middle(), block, refs[at + 1][slice(*p[-1])])
                at += len(p) - 1
                blocks.append(block)
            if key in done:
                y = own + product(joined(blocks), own_half(h, number)[1], own_half(l, number)[1])
            else:
                y = product(stacked(own, joined(blocks), bit_of(bits[number])), h[...], l[...])
            at = 0
            for o in out_refs:
                o[...] = y[at : at + o.shape[0]]
                at += o.shape[0]

        return chain(name, body, args + matrix[number], outs)

    def inside(groups, group):
        return [g for g in groups if set(g) <= set(group)]

    def step_a(i):
        group = X_GROUPS[i]
        parts = inside(S_GROUPS, group)
        out = level("level0", 0, pieces(c0, group), pieces(x, group), [rows(g) for g in parts])
        for g, c in zip(parts, out):
            c1[g] = c
            if S_GROUPS.index(g) in DIRECT:
                got[g] = send(c, across(1))
            else:
                got[g] = send(c, middle)

    def step_p(i):
        group = S_GROUPS[i]

        def body(own, other, o_ref):
            o_ref[...] = jnp.where(is_middle(), other[...], own[...])

        passed = chain("pass", body, [c1[group], got[group]], [rows(group)])[0]
        got[group] = send(passed, across(2))

    def step_q(i):
        group = S_GROUPS[i]
        kept = chain("order", lambda *_: None, [got[group]], [rows(group)], in_place=0)[0]
        got[group] = (send(kept, middle), kept)

    def step_b(i):
        group = B_GROUPS[i]
        parts = inside(Z_GROUPS, group)
        out = level(
            "level1",
            1,
            pieces(c1, group),
            pieces(got, group),
            [rows(g) for g in parts],
            ("b", i),
        )
        for g, c in zip(parts, out):
            c2[g] = c
            z[g] = send(c, across(2))

    def step_c(i):
        group = Y_GROUPS[i]
        c3[group] = level(
            "level2", 2, pieces(c2, group), pieces(z, group), [rows(group)], ("c", i)
        )[0]
        y[group] = send(c3[group], across(3))

    def step_bb(i):
        ahead(("b", i), 1, pieces(c1, B_GROUPS[i]))

    def step_cc(i):
        ahead(("c", i), 2, pieces(c2, Y_GROUPS[i]))

    def columns_of(store, j):
        first, stop = (b * unit for b in RESULT_BLOCKS[j])
        found = []
        for group in Y_GROUPS:
            begin = ends[group[0]] - sizes[group[0]]
            cut = [max(first - begin, 0), min(stop, ends[group[-1]]) - begin]
            if cut[0] < cut[1]:
                found.append((store[group], cut))
        return found

    def step_dd(j):
        ahead(("d", j), 3, columns_of(c3, j), turned=True)

    def step_d(j):
        first, stop = (b * unit for b in RESULT_BLOCKS[j])
        key = ("d", j)
        mine, other = columns_of(c3, j), columns_of(y, j)
        if key in done:
            mine = [(done[key], [0, rank])]
        args = [p[0] for p in mine + other] + matrix[3]

        def body(*refs):
            held, sem = refs[-2:]
            h, l = refs[len(mine) + len(other) : len(mine) + len(other) + 2]
            o_ref, mark = refs[-4], refs[-3]
            mark[...] = jnp.zeros_like(mark)
            own = joined([r[slice(*p[-1])] for r, p in zip(refs, mine)])
            theirs = joined([r[slice(*p[-1])] for r, p in zip(refs[len(mine) :], other)])
            copies = []
            for half in range(2):
                part = slice(half * rank // 2, (half + 1) * rank // 2)
                if key in done:
                    mh, ml = own_half(h.at[part], 3)[1], own_half(l.at[part], 3)[1]
                    held[part] = own[part] + product_t(theirs, mh, ml)
                else:
                    both = stacked(own, theirs, bit_of(bits[3]))
                    held[part] = product_t(both, h[part], l[part])
                copies.append(
                    pltpu.make_async_copy(
                        held.at[part], o_ref.at[0, part, first:stop], sem.at[half]
                    )
                )
                copies[-1].start()
            for copy in copies:
                copy.wait()

        in_place = None
        if result:
            in_place = len(args)
            args.append(result[-1])
        outs = [pltpu.HBM(coeffs.shape, F32), jax.ShapeDtypeStruct((8, 128), F32)]
        scratch = [pltpu.VMEM((rank, stop - first), F32), pltpu.SemaphoreType.DMA((2,))]
        result.append(
            chain("level3", body, args, outs, scratch, in_place=in_place, out_hbm=True)[0]
        )

    c0, x, c1, got, c2, z, c3, y, matrix, result = ({} for _ in range(10))
    result, done = [], {}
    steps = {"in": step_in, "m": step_m, "x": step_x, "a": step_a, "p": step_p}
    steps |= {"q": step_q, "b": step_b, "c": step_c, "d": step_d}
    steps |= {"bb": step_bb, "cc": step_cc, "dd": step_dd}
    for words in ORDER:
        for word in words.split():
            steps[word[:-1]](int(word[-1]))
    return result[-1]


def solution(mesh):
    placed = (P(AXES, None, None), P(None, AXES, None, None))
    return jax.shard_map(
        per_device,
        mesh=mesh,
        in_specs=placed,
        out_specs=P(AXES, None, None),
        check_vma=False,
    )
```

```python
import jax
import jax.numpy as jnp
from jax import lax
from jax.experimental import pallas as pl
from jax.experimental.pallas import tpu as pltpu
from jax.sharding import PartitionSpec as P

AXES = ("gx", "gy", "gz")
F32, BF16 = jnp.float32, jnp.bfloat16
VMEM = pl.BlockSpec(memory_space=pltpu.VMEM)
HBM = pl.BlockSpec(memory_space=pltpu.HBM)
ANY = pl.BlockSpec(memory_space=pl.ANY)
CHUNKS = (4, 6, 6, 8, 8)
X_GROUPS = ((0,), (1,), (2,), (3,), (4,))
S_GROUPS = ((0,), (1,), (2,), (3,), (4,))
B_GROUPS = ((0,), (1,), (2,), (3,), (4,))
Z_GROUPS = ((0,), (1,), (2,), (3,), (4,))
Y_GROUPS = ((0,), (1,), (2,), (3,), (4,))
DIRECT = (0,)
RESULT_BLOCKS = ((0, 3), (3, 4))
COST = 4000000000
COSTS = {'ahead': 1000000000}
ORDER = (
    "in0 x0 in1 x1",
    "x2 m0 a0 x3",
    "m1 x4 m2 a1",
    "a2 b0 p1 a3",
    "p2 a4 p3 q1",
    "p4 m3 q2 q3",
    "c0 b1 q4 b2",
    "cc1 c1 b3 cc2",
    "c2 b4 cc3 cc4",
    "c3 c4 d0 dd1",
    "d1",
)


def bit_of(bit):
    index = lax.axis_index(AXES[0])
    for axis in AXES[1:]:
        index = index * lax.axis_size(axis) + lax.axis_index(axis)
    return index >> bit & 1


def send(block, partner):
    count = lax.axis_size(AXES)
    return lax.ppermute(block, AXES, [(i, partner(i)) for i in range(count)])


def split(x):
    high = x.astype(BF16)
    return high, (x - high.astype(F32)).astype(BF16)


def dot_t(a, b):
    return lax.dot_general(a, b, (((1,), (1,)), ((), ())), preferred_element_type=F32)


def product(x, mh, ml):
    rows = x.shape[0]
    xh, xl = split(x)
    both = dot_t(jnp.concatenate([xh, xl], axis=0), mh)
    return both[:rows] + (both[rows:] + dot_t(xh, ml))


def product_t(x, mh, ml):
    rows = x.shape[0]
    xh, xl = split(x)
    both = dot_t(mh, jnp.concatenate([xh, xl], axis=0))
    return both[:, :rows] + (both[:, rows:] + dot_t(ml, xh))


def stacked(own, other, upper):
    return jnp.concatenate(
        [jnp.where(upper == 1, other, own), jnp.where(upper == 1, own, other)], axis=1
    )


def joined(blocks):
    return blocks[0] if len(blocks) == 1 else jnp.concatenate(blocks, axis=0)


class Chain:
    def __init__(self):
        self.last = None

    def __call__(self, name, body, args, outs, scratch=(), in_place=None, in_hbm=(), out_hbm=False):
        args, n = list(args), len(args)
        specs = [VMEM] * n
        for i in in_hbm:
            args[i] = pltpu.with_memory_space_constraint(args[i], pltpu.HBM)
            specs[i] = HBM
        if in_place is not None:
            specs[in_place] = HBM if out_hbm else ANY
        if self.last is not None and not any(a is self.last for a in args):
            args.append(self.last)
            specs.append(ANY)

        def kernel(*refs):
            body(*refs[:n], *refs[len(args) :])

        results = pl.pallas_call(
            kernel,
            out_shape=outs,
            in_specs=specs,
            out_specs=[HBM, VMEM] if out_hbm else [VMEM if in_place is None else ANY] * len(outs),
            scratch_shapes=scratch,
            input_output_aliases={} if in_place is None else {in_place: 0},
            compiler_params=pltpu.CompilerParams(vmem_limit_bytes=8 * 2**20),
            cost_estimate=pl.CostEstimate(
                flops=COSTS.get(name, COST), bytes_accessed=1000, transcendentals=0
            ),
            name=name,
        )(*args)
        self.last = results[-1]
        return list(results)


def per_device(coeffs, transfer):
    nbits = lax.axis_size(AXES).bit_length() - 1
    bits = [nbits - 1 - level for level in range(transfer.shape[0])]
    rank, rhs = coeffs.shape[1:]
    sizes = [c * rhs // 32 for c in CHUNKS]
    n = len(sizes)
    ends = [sum(sizes[: s + 1]) for s in range(n)]
    unit = rhs // 4
    chain = Chain()

    def rows(chunks):
        return jax.ShapeDtypeStruct((sum(sizes[k] for k in chunks), rank), F32)

    def across(level):
        return lambda i: i ^ 1 << bits[level]

    def middle(i):
        both = 1 << bits[1] | 1 << bits[2]
        return i ^ both if (i >> bits[1] ^ i >> bits[2]) & 1 else i ^ 1

    def is_middle():
        return bit_of(bits[1]) != bit_of(bits[2])

    def pieces(store, chunks):
        found = []
        for group in sorted(store):
            arrays = store[group]
            arrays = arrays if isinstance(arrays, tuple) else (arrays,)
            at = 0
            for k in group:
                if k in chunks:
                    if found and found[-1][0] is arrays[0]:
                        found[-1][-1][1] = at + sizes[k]
                    else:
                        found.append((*arrays, [at, at + sizes[k]]))
                at += sizes[k]
        return found

    def step_in(part):
        mine = [g for i, g in enumerate(X_GROUPS) if (i == 0) == (part == 0)]
        start = ends[mine[0][0]] - sizes[mine[0][0]]
        width = sum(sizes[k] for g in mine for k in g)
        low = start // 128 * 128
        high = -(-(start + width) // 128) * 128

        def fetched(c_ref, *refs):
            outs, (held, sem) = refs[:-2], refs[-2:]
            copies = []
            for half in range(2):
                part = slice(half * rank // 2, (half + 1) * rank // 2)
                copies.append(
                    pltpu.make_async_copy(
                        c_ref.at[0, part, low:high], held.at[part], sem.at[half]
                    )
                )
                copies[half].start()
            for half in range(2):
                part = slice(half * rank // 2, (half + 1) * rank // 2)
                copies[half].wait()
                at = start - low
                for o_ref in outs:
                    o_ref[:, part] = held[part, at : at + o_ref.shape[0]].T
                    at += o_ref.shape[0]

        def whole(c_ref, *outs):
            lay(c_ref[0], start, outs)

        def lay(block, at, outs):
            for o_ref in outs:
                o_ref[...] = block[:, at : at + o_ref.shape[0]].T
                at += o_ref.shape[0]

        scratch = [pltpu.VMEM((rank, high - low), F32), pltpu.SemaphoreType.DMA((2,))]
        out = chain(
            "columns",
            whole if part else fetched,
            [coeffs],
            [rows(g) for g in mine],
            scratch=[] if part else scratch,
            in_hbm=[] if part else [0],
        )
        c0.update(zip(mine, out))

    def step_m(level):
        def body(t_ref, h_ref, l_ref):
            h_ref[...], l_ref[...] = split(t_ref[level, 0])

        matrix[level] = chain(
            "matrix",
            body,
            [transfer],
            [jax.ShapeDtypeStruct((rank, 2 * rank), BF16)] * 2,
        )

    def step_x(i):
        group = X_GROUPS[i]
        c0[group] = chain("order", lambda *_: None, [c0[group]], [rows(group)], in_place=0)[0]
        x[group] = send(c0[group], across(0))

    def own_half(ref, number):
        upper = bit_of(bits[number])
        own = ref[:, pl.ds(pl.multiple_of(upper * rank, rank), rank)]
        return own, ref[:, pl.ds(pl.multiple_of((1 - upper) * rank, rank), rank)]

    def ahead(key, number, mine, turned=False):
        args = [p[0] for p in mine]
        size = sum(p[-1][1] - p[-1][0] for p in mine)

        def body(*refs):
            h, l, o = refs[len(args) :]
            own = joined([r[slice(*p[-1])] for r, p in zip(refs, mine)])
            times = product_t if turned else product
            o[...] = times(own, own_half(h, number)[0], own_half(l, number)[0])

        shape = (rank, size) if turned else (size, rank)
        outs = [jax.ShapeDtypeStruct(shape, F32)]
        done[key] = chain("ahead", body, args + matrix[number], outs)[0]

    def level(name, number, mine, other, outs, key=None):
        if key in done:
            mine = [(done[key], [0, sum(p[-1][1] - p[-1][0] for p in mine)])]
        args = [p[0] for p in mine] + [a for p in other for a in p[:-1]]

        def body(*refs):
            out_refs = refs[len(args) + 2 :]
            h, l = refs[len(args) : len(args) + 2]
            own = joined([r[slice(*p[-1])] for r, p in zip(refs, mine)])
            at, blocks = len(mine), []
            for p in other:
                block = refs[at][slice(*p[-1])]
                if len(p) == 3:
                    block = jnp.where(is_middle(), block, refs[at + 1][slice(*p[-1])])
                at += len(p) - 1
                blocks.append(block)
            if key in done:
                y = own + product(joined(blocks), own_half(h, number)[1], own_half(l, number)[1])
            else:
                y = product(stacked(own, joined(blocks), bit_of(bits[number])), h[...], l[...])
            at = 0
            for o in out_refs:
                o[...] = y[at : at + o.shape[0]]
                at += o.shape[0]

        return chain(name, body, args + matrix[number], outs)

    def inside(groups, group):
        return [g for g in groups if set(g) <= set(group)]

    def step_a(i):
        group = X_GROUPS[i]
        parts = inside(S_GROUPS, group)
        out = level("level0", 0, pieces(c0, group), pieces(x, group), [rows(g) for g in parts])
        for g, c in zip(parts, out):
            c1[g] = c
            if S_GROUPS.index(g) in DIRECT:
                got[g] = send(c, across(1))
            else:
                got[g] = send(c, middle)

    def step_p(i):
        group = S_GROUPS[i]

        def body(own, other, o_ref):
            o_ref[...] = jnp.where(is_middle(), other[...], own[...])

        passed = chain("pass", body, [c1[group], got[group]], [rows(group)])[0]
        got[group] = send(passed, across(2))

    def step_q(i):
        group = S_GROUPS[i]
        kept = chain("order", lambda *_: None, [got[group]], [rows(group)], in_place=0)[0]
        got[group] = (send(kept, middle), kept)

    def step_b(i):
        group = B_GROUPS[i]
        parts = inside(Z_GROUPS, group)
        out = level(
            "level1",
            1,
            pieces(c1, group),
            pieces(got, group),
            [rows(g) for g in parts],
            ("b", i),
        )
        for g, c in zip(parts, out):
            c2[g] = c
            z[g] = send(c, across(2))

    def step_c(i):
        group = Y_GROUPS[i]
        c3[group] = level(
            "level2", 2, pieces(c2, group), pieces(z, group), [rows(group)], ("c", i)
        )[0]
        y[group] = send(c3[group], across(3))

    def step_bb(i):
        ahead(("b", i), 1, pieces(c1, B_GROUPS[i]))

    def step_cc(i):
        ahead(("c", i), 2, pieces(c2, Y_GROUPS[i]))

    def columns_of(store, j):
        first, stop = (b * unit for b in RESULT_BLOCKS[j])
        found = []
        for group in Y_GROUPS:
            begin = ends[group[0]] - sizes[group[0]]
            cut = [max(first - begin, 0), min(stop, ends[group[-1]]) - begin]
            if cut[0] < cut[1]:
                found.append((store[group], cut))
        return found

    def step_dd(j):
        ahead(("d", j), 3, columns_of(c3, j), turned=True)

    def step_d(j):
        first, stop = (b * unit for b in RESULT_BLOCKS[j])
        key = ("d", j)
        mine, other = columns_of(c3, j), columns_of(y, j)
        if key in done:
            mine = [(done[key], [0, rank])]
        args = [p[0] for p in mine + other] + matrix[3]

        def body(*refs):
            held, sem = refs[-2:]
            h, l = refs[len(mine) + len(other) : len(mine) + len(other) + 2]
            o_ref, mark = refs[-4], refs[-3]
            mark[...] = jnp.zeros_like(mark)
            own = joined([r[slice(*p[-1])] for r, p in zip(refs, mine)])
            theirs = joined([r[slice(*p[-1])] for r, p in zip(refs[len(mine) :], other)])
            copies = []
            for half in range(2):
                part = slice(half * rank // 2, (half + 1) * rank // 2)
                if key in done:
                    mh, ml = own_half(h.at[part], 3)[1], own_half(l.at[part], 3)[1]
                    held[part] = own[part] + product_t(theirs, mh, ml)
                else:
                    both = stacked(own, theirs, bit_of(bits[3]))
                    held[part] = product_t(both, h[part], l[part])
                copies.append(
                    pltpu.make_async_copy(
                        held.at[part], o_ref.at[0, part, first:stop], sem.at[half]
                    )
                )
                copies[-1].start()
            for copy in copies:
                copy.wait()

        in_place = None
        if result:
            in_place = len(args)
            args.append(result[-1])
        outs = [pltpu.HBM(coeffs.shape, F32), jax.ShapeDtypeStruct((8, 128), F32)]
        scratch = [pltpu.VMEM((rank, stop - first), F32), pltpu.SemaphoreType.DMA((2,))]
        result.append(
            chain("level3", body, args, outs, scratch, in_place=in_place, out_hbm=True)[0]
        )

    c0, x, c1, got, c2, z, c3, y, matrix, result = ({} for _ in range(10))
    result, done = [], {}
    steps = {"in": step_in, "m": step_m, "x": step_x, "a": step_a, "p": step_p}
    steps |= {"q": step_q, "b": step_b, "c": step_c, "d": step_d}
    steps |= {"bb": step_bb, "cc": step_cc, "dd": step_dd}
    for words in ORDER:
        for word in words.split():
            steps[word[:-1]](int(word[-1]))
    return result[-1]


def solution(mesh):
    placed = (P(AXES, None, None), P(None, AXES, None, None))
    return jax.shard_map(
        per_device,
        mesh=mesh,
        in_specs=placed,
        out_specs=P(AXES, None, None),
        check_vma=False,
    )
```

```python
import jax
import jax.numpy as jnp
from jax import lax
from jax.experimental import pallas as pl
from jax.experimental.pallas import tpu as pltpu
from jax.sharding import PartitionSpec as P

AXES = ("gx", "gy", "gz")
F32, BF16 = jnp.float32, jnp.bfloat16
VMEM = pl.BlockSpec(memory_space=pltpu.VMEM)
HBM = pl.BlockSpec(memory_space=pltpu.HBM)
ANY = pl.BlockSpec(memory_space=pl.ANY)
CHUNKS = (4, 6, 6, 8, 8)
X_GROUPS = ((0,), (1,), (2,), (3,), (4,))
S_GROUPS = ((0,), (1,), (2,), (3,), (4,))
B_GROUPS = ((0,), (1,), (2,), (3,), (4,))
Z_GROUPS = ((0,), (1,), (2,), (3,), (4,))
Y_GROUPS = ((0,), (1,), (2,), (3,), (4,))
DIRECT = (0,)
RESULT_BLOCKS = ((0, 3), (3, 4))
COST = 4000000000
COSTS = {'ahead': 1000000000}
ORDER = (
    "in0 x0 in1 x1",
    "x2 m0 a0 x3",
    "m1 x4 m2 a1",
    "a2 b0 p1 a3",
    "p2 a4 p3 q1",
    "p4 m3 q2 q3",
    "c0 b1 q4 b2",
    "cc1 c1 b3 cc2",
    "c2 b4 cc3 cc4",
    "c3 c4 d0 dd1",
    "d1",
)


def bit_of(bit):
    index = lax.axis_index(AXES[0])
    for axis in AXES[1:]:
        index = index * lax.axis_size(axis) + lax.axis_index(axis)
    return index >> bit & 1


def send(block, partner):
    count = lax.axis_size(AXES)
    return lax.ppermute(block, AXES, [(i, partner(i)) for i in range(count)])


def split(x):
    high = x.astype(BF16)
    return high, (x - high.astype(F32)).astype(BF16)


def dot_t(a, b):
    return lax.dot_general(a, b, (((1,), (1,)), ((), ())), preferred_element_type=F32)


def product(x, mh, ml):
    rows = x.shape[0]
    xh, xl = split(x)
    both = dot_t(jnp.concatenate([xh, xl], axis=0), mh)
    return both[:rows] + (both[rows:] + dot_t(xh, ml))


def product_t(x, mh, ml):
    rows = x.shape[0]
    xh, xl = split(x)
    both = dot_t(mh, jnp.concatenate([xh, xl], axis=0))
    return both[:, :rows] + (both[:, rows:] + dot_t(ml, xh))


def stacked(own, other, upper):
    return jnp.concatenate(
        [jnp.where(upper == 1, other, own), jnp.where(upper == 1, own, other)], axis=1
    )


def joined(blocks):
    return blocks[0] if len(blocks) == 1 else jnp.concatenate(blocks, axis=0)


class Chain:
    def __init__(self):
        self.last = None

    def __call__(self, name, body, args, outs, scratch=(), in_place=None, in_hbm=(), out_hbm=False):
        args, n = list(args), len(args)
        specs = [VMEM] * n
        for i in in_hbm:
            args[i] = pltpu.with_memory_space_constraint(args[i], pltpu.HBM)
            specs[i] = HBM
        if in_place is not None:
            specs[in_place] = HBM if out_hbm else ANY
        if self.last is not None and not any(a is self.last for a in args):
            args.append(self.last)
            specs.append(ANY)

        def kernel(*refs):
            body(*refs[:n], *refs[len(args) :])

        results = pl.pallas_call(
            kernel,
            out_shape=outs,
            in_specs=specs,
            out_specs=[HBM, VMEM] if out_hbm else [VMEM if in_place is None else ANY] * len(outs),
            scratch_shapes=scratch,
            input_output_aliases={} if in_place is None else {in_place: 0},
            compiler_params=pltpu.CompilerParams(vmem_limit_bytes=8 * 2**20),
            cost_estimate=pl.CostEstimate(
                flops=COSTS.get(name, COST), bytes_accessed=1000, transcendentals=0
            ),
            name=name,
        )(*args)
        self.last = results[-1]
        return list(results)


def per_device(coeffs, transfer):
    nbits = lax.axis_size(AXES).bit_length() - 1
    bits = [nbits - 1 - level for level in range(transfer.shape[0])]
    rank, rhs = coeffs.shape[1:]
    sizes = [c * rhs // 32 for c in CHUNKS]
    n = len(sizes)
    ends = [sum(sizes[: s + 1]) for s in range(n)]
    unit = rhs // 4
    chain = Chain()

    def rows(chunks):
        return jax.ShapeDtypeStruct((sum(sizes[k] for k in chunks), rank), F32)

    def across(level):
        return lambda i: i ^ 1 << bits[level]

    def middle(i):
        both = 1 << bits[1] | 1 << bits[2]
        return i ^ both if (i >> bits[1] ^ i >> bits[2]) & 1 else i ^ 1

    def is_middle():
        return bit_of(bits[1]) != bit_of(bits[2])

    def pieces(store, chunks):
        found = []
        for group in sorted(store):
            arrays = store[group]
            arrays = arrays if isinstance(arrays, tuple) else (arrays,)
            at = 0
            for k in group:
                if k in chunks:
                    if found and found[-1][0] is arrays[0]:
                        found[-1][-1][1] = at + sizes[k]
                    else:
                        found.append((*arrays, [at, at + sizes[k]]))
                at += sizes[k]
        return found

    def step_in(part):
        mine = [g for i, g in enumerate(X_GROUPS) if (i == 0) == (part == 0)]
        start = ends[mine[0][0]] - sizes[mine[0][0]]
        width = sum(sizes[k] for g in mine for k in g)
        low = start // 128 * 128
        high = -(-(start + width) // 128) * 128

        def fetched(c_ref, *refs):
            outs, (held, sem) = refs[:-2], refs[-2:]
            copies = []
            for half in range(2):
                part = slice(half * rank // 2, (half + 1) * rank // 2)
                copies.append(
                    pltpu.make_async_copy(
                        c_ref.at[0, part, low:high], held.at[part], sem.at[half]
                    )
                )
                copies[half].start()
            for half in range(2):
                part = slice(half * rank // 2, (half + 1) * rank // 2)
                copies[half].wait()
                at = start - low
                for o_ref in outs:
                    o_ref[:, part] = held[part, at : at + o_ref.shape[0]].T
                    at += o_ref.shape[0]

        def whole(c_ref, *outs):
            lay(c_ref[0], start, outs)

        def lay(block, at, outs):
            for o_ref in outs:
                o_ref[...] = block[:, at : at + o_ref.shape[0]].T
                at += o_ref.shape[0]

        scratch = [pltpu.VMEM((rank, high - low), F32), pltpu.SemaphoreType.DMA((2,))]
        out = chain(
            "columns",
            whole if part else fetched,
            [coeffs],
            [rows(g) for g in mine],
            scratch=[] if part else scratch,
            in_hbm=[] if part else [0],
        )
        c0.update(zip(mine, out))

    def step_m(level):
        def body(t_ref, h_ref, l_ref):
            h_ref[...], l_ref[...] = split(t_ref[level, 0])

        matrix[level] = chain(
            "matrix",
            body,
            [transfer],
            [jax.ShapeDtypeStruct((rank, 2 * rank), BF16)] * 2,
        )

    def step_x(i):
        group = X_GROUPS[i]
        c0[group] = chain("order", lambda *_: None, [c0[group]], [rows(group)], in_place=0)[0]
        x[group] = send(c0[group], across(0))

    def own_half(ref, number):
        upper = bit_of(bits[number])
        own = ref[:, pl.ds(pl.multiple_of(upper * rank, rank), rank)]
        return own, ref[:, pl.ds(pl.multiple_of((1 - upper) * rank, rank), rank)]

    def ahead(key, number, mine, turned=False):
        args = [p[0] for p in mine]
        size = sum(p[-1][1] - p[-1][0] for p in mine)

        def body(*refs):
            h, l, o = refs[len(args) :]
            own = joined([r[slice(*p[-1])] for r, p in zip(refs, mine)])
            times = product_t if turned else product
            o[...] = times(own, own_half(h, number)[0], own_half(l, number)[0])

        shape = (rank, size) if turned else (size, rank)
        outs = [jax.ShapeDtypeStruct(shape, F32)]
        done[key] = chain("ahead", body, args + matrix[number], outs)[0]

    def level(name, number, mine, other, outs, key=None):
        if key in done:
            mine = [(done[key], [0, sum(p[-1][1] - p[-1][0] for p in mine)])]
        args = [p[0] for p in mine] + [a for p in other for a in p[:-1]]

        def body(*refs):
            out_refs = refs[len(args) + 2 :]
            h, l = refs[len(args) : len(args) + 2]
            own = joined([r[slice(*p[-1])] for r, p in zip(refs, mine)])
            at, blocks = len(mine), []
            for p in other:
                block = refs[at][slice(*p[-1])]
                if len(p) == 3:
                    block = jnp.where(is_middle(), block, refs[at + 1][slice(*p[-1])])
                at += len(p) - 1
                blocks.append(block)
            if key in done:
                y = own + product(joined(blocks), own_half(h, number)[1], own_half(l, number)[1])
            else:
                y = product(stacked(own, joined(blocks), bit_of(bits[number])), h[...], l[...])
            at = 0
            for o in out_refs:
                o[...] = y[at : at + o.shape[0]]
                at += o.shape[0]

        return chain(name, body, args + matrix[number], outs)

    def inside(groups, group):
        return [g for g in groups if set(g) <= set(group)]

    def step_a(i):
        group = X_GROUPS[i]
        parts = inside(S_GROUPS, group)
        out = level("level0", 0, pieces(c0, group), pieces(x, group), [rows(g) for g in parts])
        for g, c in zip(parts, out):
            c1[g] = c
            if S_GROUPS.index(g) in DIRECT:
                got[g] = send(c, across(1))
            else:
                got[g] = send(c, middle)

    def step_p(i):
        group = S_GROUPS[i]

        def body(own, other, o_ref):
            o_ref[...] = jnp.where(is_middle(), other[...], own[...])

        passed = chain("pass", body, [c1[group], got[group]], [rows(group)])[0]
        got[group] = send(passed, across(2))

    def step_q(i):
        group = S_GROUPS[i]
        kept = chain("order", lambda *_: None, [got[group]], [rows(group)], in_place=0)[0]
        got[group] = (send(kept, middle), kept)

    def step_b(i):
        group = B_GROUPS[i]
        parts = inside(Z_GROUPS, group)
        out = level(
            "level1",
            1,
            pieces(c1, group),
            pieces(got, group),
            [rows(g) for g in parts],
            ("b", i),
        )
        for g, c in zip(parts, out):
            c2[g] = c
            z[g] = send(c, across(2))

    def step_c(i):
        group = Y_GROUPS[i]
        c3[group] = level(
            "level2", 2, pieces(c2, group), pieces(z, group), [rows(group)], ("c", i)
        )[0]
        y[group] = send(c3[group], across(3))

    def step_bb(i):
        ahead(("b", i), 1, pieces(c1, B_GROUPS[i]))

    def step_cc(i):
        ahead(("c", i), 2, pieces(c2, Y_GROUPS[i]))

    def columns_of(store, j):
        first, stop = (b * unit for b in RESULT_BLOCKS[j])
        found = []
        for group in Y_GROUPS:
            begin = ends[group[0]] - sizes[group[0]]
            cut = [max(first - begin, 0), min(stop, ends[group[-1]]) - begin]
            if cut[0] < cut[1]:
                found.append((store[group], cut))
        return found

    def step_dd(j):
        ahead(("d", j), 3, columns_of(c3, j), turned=True)

    def step_d(j):
        first, stop = (b * unit for b in RESULT_BLOCKS[j])
        key = ("d", j)
        mine, other = columns_of(c3, j), columns_of(y, j)
        if key in done:
            mine = [(done[key], [0, rank])]
        args = [p[0] for p in mine + other] + matrix[3]

        def body(*refs):
            held, sem = refs[-2:]
            h, l = refs[len(mine) + len(other) : len(mine) + len(other) + 2]
            o_ref, mark = refs[-4], refs[-3]
            mark[...] = jnp.zeros_like(mark)
            own = joined([r[slice(*p[-1])] for r, p in zip(refs, mine)])
            theirs = joined([r[slice(*p[-1])] for r, p in zip(refs[len(mine) :], other)])
            copies = []
            for half, part in enumerate((slice(0, 3 * rank // 4), slice(3 * rank // 4, rank))):
                if key in done:
                    mh, ml = own_half(h.at[part], 3)[1], own_half(l.at[part], 3)[1]
                    held[part] = own[part] + product_t(theirs, mh, ml)
                else:
                    both = stacked(own, theirs, bit_of(bits[3]))
                    held[part] = product_t(both, h[part], l[part])
                copies.append(
                    pltpu.make_async_copy(
                        held.at[part], o_ref.at[0, part, first:stop], sem.at[half]
                    )
                )
                copies[-1].start()
            for copy in copies:
                copy.wait()

        in_place = None
        if result:
            in_place = len(args)
            args.append(result[-1])
        outs = [pltpu.HBM(coeffs.shape, F32), jax.ShapeDtypeStruct((8, 128), F32)]
        scratch = [pltpu.VMEM((rank, stop - first), F32), pltpu.SemaphoreType.DMA((2,))]
        result.append(
            chain("level3", body, args, outs, scratch, in_place=in_place, out_hbm=True)[0]
        )

    c0, x, c1, got, c2, z, c3, y, matrix, result = ({} for _ in range(10))
    result, done = [], {}
    steps = {"in": step_in, "m": step_m, "x": step_x, "a": step_a, "p": step_p}
    steps |= {"q": step_q, "b": step_b, "c": step_c, "d": step_d}
    steps |= {"bb": step_bb, "cc": step_cc, "dd": step_dd}
    for words in ORDER:
        for word in words.split():
            steps[word[:-1]](int(word[-1]))
    return result[-1]


def solution(mesh):
    placed = (P(AXES, None, None), P(None, AXES, None, None))
    return jax.shard_map(
        per_device,
        mesh=mesh,
        in_specs=placed,
        out_specs=P(AXES, None, None),
        check_vma=False,
    )
```
